32 devices in a mesh: groups: 2 (over x), pts: 8 (over z, y), branch: 2 (over core).
Axes of the slice: x: 2, y: 2, z: 4, core: 2. Of those that a mesh axis runs over, the one named last changes fastest.
Arguments:
- point_feat: bfloat16 [2, 65536, 128], P('branch', ('groups', 'pts')), parts along dimension 1, may hold values from -6 to 6
- query_feat: bfloat16 [2, 8192, 768], P('branch', ('groups', 'pts')), parts along dimension 1, may hold values from -640 to 640
- supernode_query: bfloat16 [2, 512, 768], P('branch', ('groups', 'pts')), parts along dimension 1, may hold values from -1000 to 1000
- route_owner: int32 [2, 512, 1], P('branch', 'groups'), parts along dimension 1, may hold values from 0 to 7; in each aligned block of 32 rows (0 to 31, 32 to 63, ..., all dimensions but the last counted through in order) at most 8 rows name the same one
- route_slot: int32 [2, 512], P('branch', 'groups'), parts along dimension 1, may hold values from 0 to 31
- anchor_index: int32 [2, 384], P('branch', 'groups'), parts along dimension 1, may hold values from 0 to 255, as said below
- w_in: bfloat16 [2, 128, 768], P('branch'), may hold values from -0.5 to 0.5
- w_mid: bfloat16 [2, 768, 768], P('branch'), may hold values from -0.21875 to 0.21875
- w_q: bfloat16 [2, 768, 768], P('branch'), may hold values from -0.21875 to 0.21875
- w_kv: bfloat16 [2, 768, 1536], P('branch'), may hold values from -0.21875 to 0.21875
- w_out: bfloat16 [2, 1536, 768], P('branch'), may hold values from -1.25 to 1.25
Outputs:
- result: bfloat16 [2, 8192, 768], P('branch', ('groups', 'pts')), parts along dimension 1
The draws below stay inside these ranges and needn't reach their ends.
There are 2 independent parts, one for each index of `groups`. The reference program is written for one: setup_inputs(seed, part) draws one part's arguments, and reference() takes and returns one part's arrays. A program takes and returns all parts, laid end to end along the dimension named above; an argument that names none is the same for every part. Nothing has to cross between parts.
Inputs may be any that keep to these rules, and one draw needn't show every extreme that they name: `route_owner`: within the rows of one device, at most 8 blocks name one owner, and in every draw some device sends exactly 8 blocks to one owner. `anchor_index`: the 192 entries of each branch are distinct.
All inputs are finite; a program needn't handle non-finite values.
Results may differ from the reference program's by a relative error of at most 0.014.
The reference program's roundings to bfloat16 on the way count: a program that leaves them out, or rounds other values in their place, can miss the bound.
Values may be sent and summed in bfloat16 or wider, within the bound.
A program may use at most 128 MiB of HBM per device.

```python
import math
import jax
import jax.numpy as jnp
import numpy as np
from jax import lax

D = 768
HEADS = 12
F_IN = 128
BLK = 128
NB_DEV = 32
SN_DEV = 32
ANC_DEV = 24
Q_DEV = 512
CAP = 8
POINTS = 32768
NBLOCKS = 256
N_PTS = 8


def scaled_rows(key, rows):
    base = jax.random.truncated_normal(jax.random.fold_in(key, 11), -4.0, 4.0, (2, rows, D), jnp.float32)
    return base.astype(jnp.bfloat16)


def draw_query_feat(key, part):
    return scaled_rows(jax.random.fold_in(key, 21), Q_DEV * N_PTS)


def draw_supernode_query(key, part):
    return scaled_rows(jax.random.fold_in(key, 31), SN_DEV * N_PTS)


def draw_anchor_index(key, part):
    first = jax.random.permutation(jax.random.fold_in(key, 41), SN_DEV * N_PTS)[:ANC_DEV * N_PTS]
    second = jax.random.permutation(jax.random.fold_in(key, 42), SN_DEV * N_PTS)[:ANC_DEV * N_PTS]
    return jnp.stack([first, second], axis=0).astype(jnp.int32)


def touch_ends(result, key, least, high):
    longest = result.shape.index(max(result.shape))
    spots = []
    for shift in (0, 1):
        where = [jax.random.randint(jax.random.fold_in(key, axis), (), 0, length) for axis, length in enumerate(result.shape)]
        where[longest] = (where[longest] + shift) % result.shape[longest]
        spots.append(tuple(where))
    return result.at[spots[0]].set(least).at[spots[1]].set(high)


def block_levels(own_key, extent, cuts, smallest, largest):
    level, own = 1.0, jax.random.fold_in(own_key, 6)
    for position, parts in cuts:
        draws = jnp.exp(jax.random.uniform(jax.random.fold_in(own, position), (parts,), jnp.float32, smallest / len(cuts), largest / len(cuts)))
        level = level * jnp.repeat(draws, extent[position] // parts).reshape([-1 if axis == position else 1 for axis in range(len(extent))])
    return level


def routed_block(rng, own, number, rows, number_of, top, limit, lean):
    order = jax.random.permutation(rng, number_of)
    crowded, usual = load_shares(number_of, rows * top, limit, lean, True), load_shares(number_of, rows * top, limit, lean, False)
    places = jnp.arange(number_of)

    def named(lengths, turn):
        used = int((lengths > 0).sum())
        fixed = max(1, used // 4)
        moved = fixed + (places - fixed + turn * (used - fixed)) % max(1, number_of - fixed)
        return jnp.zeros((number_of,), jnp.int32).at[order[jnp.where(places < fixed, places, moved)]].set(jnp.asarray(lengths, jnp.int32))

    lengths = jnp.where(number % 4 == 0, named(crowded, number // 4), named(usual, number - number // 4 - 1))
    mixed = jax.random.permutation(jax.random.fold_in(own, 3), number_of)
    donor, receiver = mixed[0:number_of // 2 * 2:2], mixed[1:number_of // 2 * 2:2]
    room = jnp.minimum(lengths[donor] - 1, limit - lengths[receiver]) // 2
    room = jnp.where((donor == order[0]) | (receiver == order[0]) | (lengths[receiver] == 0), 0, jnp.maximum(room, 0))
    moved = jax.random.randint(jax.random.fold_in(own, 4), (number_of // 2,), 0, 1 << 20) % (room + 1)
    lengths = lengths.at[donor].add(-moved).at[receiver].add(moved)
    members = jnp.searchsorted(jnp.cumsum(lengths), jnp.arange(rows * top), side="right").astype(jnp.int32)
    grid = members.reshape(top, rows).T
    grid = grid[jax.random.permutation(jax.random.fold_in(own, 1), rows)]
    turn = jax.random.randint(jax.random.fold_in(own, 2), (rows, 1), 0, top)
    return jnp.take_along_axis(grid, (jnp.arange(top)[None, :] + turn) % top, axis=1)


def load_shares(number_of, total, most, slope, full):
    weights = [(1 << 20) // math.isqrt(rank ** slope) + 1 for rank in range(1, number_of + 1)]
    largest = most if full else min(most, max(-(-total // number_of), total * weights[0] // sum(weights)))
    least = 1 if total - largest >= number_of - 1 else 0
    holding, surplus = [largest] + [least] * (number_of - 1), total - largest - least * (number_of - 1)
    while surplus > 0:
        free = [i for i in range(1, number_of) if holding[i] < largest] or [i for i in range(1, number_of) if holding[i] < most]
        mass, budget = sum([weights[i] for i in free]), surplus
        for i in free:
            extra = min(most - holding[i], max(1, budget * weights[i] // mass), surplus)
            holding[i] = holding[i] + extra
            surplus = surplus - extra
    return np.array(holding)


def centred(own_key, shape, deviation, bound, cuts=(), held_as=jnp.bfloat16):
    values = deviation * jax.random.normal(own_key, shape, jnp.float32)
    if cuts:
        values = values * block_levels(own_key, shape, cuts, -0.22, 0.18)
    return jnp.clip(values, -bound, bound).astype(held_as)


def setup_inputs(seed: int = 0, part: int = 0) -> dict:
    splits = jax.random.split(jax.random.key(seed), 12)
    part_splits = jax.random.split(jax.random.fold_in(splits[11], part), 12)
    point_feat = centred(part_splits[0], (2, POINTS, F_IN), 1.0, 6.0, ((0, 2), (1, 8)))
    query_feat = draw_query_feat(jax.random.fold_in(jax.random.fold_in(splits[11], part), 71), part)
    supernode_query = draw_supernode_query(jax.random.fold_in(jax.random.fold_in(splits[11], part), 71), part)
    route_owner_keys = jax.random.split(jax.random.fold_in(part_splits[3], 1), 2 * NBLOCKS // NB_DEV)
    route_owner_turns = jax.random.permutation(jax.random.fold_in(part_splits[3], 3), 2 * NBLOCKS // NB_DEV)
    route_owner = jax.vmap(lambda own, number: routed_block(jax.random.fold_in(part_splits[3], 2), own, number, NB_DEV, N_PTS, 1, CAP, 2))(route_owner_keys, route_owner_turns).reshape((2, NBLOCKS, 1))
    route_slot = touch_ends(jax.random.randint(part_splits[4], (2, NBLOCKS), 0, SN_DEV), jax.random.fold_in(part_splits[4], 1), 0, SN_DEV - 1).astype(jnp.int32)
    anchor_index = draw_anchor_index(jax.random.fold_in(jax.random.fold_in(splits[11], part), 71), part)
    w_in = centred(splits[6], (2, F_IN, D), F_IN ** -0.5, 0.5, ((0, 2),))
    w_mid = centred(splits[7], (2, D, D), D ** -0.5, 0.21875, ((0, 2),))
    w_q = centred(splits[8], (2, D, D), D ** -0.5, 0.21875, ((0, 2),))
    w_kv = centred(splits[9], (2, D, 2 * D), D ** -0.5, 0.21875, ((0, 2),))
    w_out = centred(splits[10], (2, 2 * D, D), (D // 32) ** -0.5, 1.25, ((0, 2),))
    return dict(point_feat=point_feat, query_feat=query_feat, supernode_query=supernode_query, route_owner=route_owner, route_slot=route_slot, anchor_index=anchor_index, w_in=w_in, w_mid=w_mid, w_q=w_q, w_kv=w_kv, w_out=w_out)


def pool_ref(blocks, queries):
    head_size = D // HEADS
    split_rows = blocks.astype(jnp.float32).reshape(blocks.shape[0], BLK, HEADS, head_size)
    asked_rows = queries.astype(jnp.float32).reshape(queries.shape[0], HEADS, head_size)
    scores = jnp.einsum('nrhe,nhe->nhr', split_rows, asked_rows) / math.sqrt(head_size)
    weights = jax.nn.softmax(scores, axis=-1).astype(jnp.bfloat16).astype(jnp.float32)
    pooled = jnp.einsum('nhr,nrhe->nhe', weights, split_rows)
    return pooled.astype(jnp.bfloat16).reshape(blocks.shape[0], D)

def attend_ref(queries, key_rows, value_rows):
    head_size = D // HEADS
    query_heads = queries.astype(jnp.float32).reshape(queries.shape[0], HEADS, head_size)
    key_heads = key_rows.astype(jnp.float32).reshape(key_rows.shape[0], HEADS, head_size)
    value_heads = value_rows.astype(jnp.float32).reshape(value_rows.shape[0], HEADS, head_size)
    scores = jnp.einsum('qhe,khe->hqk', query_heads, key_heads) / math.sqrt(head_size)
    weights = jax.nn.softmax(scores, axis=-1).astype(jnp.bfloat16).astype(jnp.float32)
    output = jnp.einsum('hqk,khe->qhe', weights, value_heads)
    return output.astype(jnp.bfloat16).reshape(queries.shape[0], D)

def reference(point_feat, query_feat, supernode_query, route_owner, route_slot, anchor_index, w_in, w_mid, w_q, w_kv, w_out):
    anchor_sets = []
    for branch in range(2):
        hidden = jax.nn.gelu(jnp.dot(point_feat[branch], w_in[branch], preferred_element_type=jnp.float32)).astype(jnp.bfloat16)
        encoded = jnp.dot(hidden, w_mid[branch], preferred_element_type=jnp.float32).astype(jnp.bfloat16)
        node_ids = (route_owner[branch, :, 0] * SN_DEV + route_slot[branch]).astype(jnp.int32)
        block_queries = jnp.take(supernode_query[branch], node_ids, axis=0)
        pooled = lax.map(lambda pair: pool_ref(pair[0], pair[1]), (encoded.reshape(N_PTS, NB_DEV, BLK, D), block_queries.reshape(N_PTS, NB_DEV, D)))
        pooled = pooled.reshape(N_PTS * NB_DEV, D)
        all_ids = jnp.arange(SN_DEV * N_PTS, dtype=jnp.int32)
        member = (node_ids[None, :] == all_ids[:, None]).astype(jnp.float32)
        pooled_sum = jnp.dot(member, pooled.astype(jnp.float32), precision=lax.Precision.HIGHEST)
        node_count = lax.optimization_barrier(jnp.sum(member, axis=1))
        combined = supernode_query[branch].astype(jnp.float32) + pooled_sum / jnp.maximum(node_count, 1.0)[:, None]
        node_feat = (combined * lax.rsqrt(lax.optimization_barrier(jnp.mean(combined * combined, axis=1, keepdims=True)) + 1e-06)).astype(jnp.bfloat16)
        anchor_rows = jnp.take(node_feat, anchor_index[branch].astype(jnp.int32), axis=0)
        anchor_sets.append(jnp.dot(anchor_rows, w_kv[branch], preferred_element_type=jnp.float32).astype(jnp.bfloat16))
    outputs = []
    query_count = Q_DEV * N_PTS
    query_step = min(512, Q_DEV)
    for branch in range(2):
        queries = jnp.dot(query_feat[branch], w_q[branch], preferred_element_type=jnp.float32).astype(jnp.bfloat16)
        own_kv = anchor_sets[branch]
        far_kv = anchor_sets[1 - branch]

        def answer(query_rows, own_kv=own_kv, far_kv=far_kv):
            self_out = attend_ref(query_rows, own_kv[:, :D], own_kv[:, D:])
            cross_out = attend_ref(query_rows, far_kv[:, :D], far_kv[:, D:])
            return jnp.concatenate([self_out, cross_out], axis=1)
        joined = lax.map(answer, queries.reshape(query_count // query_step, query_step, D)).reshape(query_count, 2 * D)
        outputs.append(jnp.dot(joined, w_out[branch], preferred_element_type=jnp.float32).astype(jnp.bfloat16))
    return jnp.stack(outputs, axis=0)
```

```python
import functools
import math

import jax
import jax.numpy as jnp
from jax import lax
from jax.experimental import pallas as pl
from jax.experimental.pallas import tpu as pltpu
from jax.sharding import PartitionSpec as P

D = 768
HEADS = 12
BLK = 128
HS = D // HEADS
LANES = 128
HP = 16
BF = jnp.bfloat16
F32 = jnp.float32
MESH = pl.DeviceIdType.MESH


def nn(a, b):
    return lax.dot_general(a, b, (((1,), (0,)), ((), ())), preferred_element_type=F32)


def nt(a, b):
    return lax.dot_general(a, b, (((1,), (1,)), ((), ())), preferred_element_type=F32)


def iota(shape, axis):
    return lax.broadcasted_iota(jnp.int32, shape, axis)


def kernel(
    shards,
    sq_ref,
    owner_ref,
    slot_ref,
    anchor_ref,
    w_in_ref,
    pf_hbm,
    qf_hbm,
    w_q_hbm,
    w_mid_hbm,
    w_kv_hbm,
    w_out_hbm,
    out_ref,
    pf,
    qf,
    w_q,
    w_mid,
    w_kv,
    w_out,
    hid,
    queries,
    all_q,
    all_p,
    u_s,
    s_s,
    g_s,
    kv_own,
    kv_far,
    joined,
    load_sem,
    q_send,
    q_recv,
    p_send,
    p_recv,
    kv_send,
    kv_recv,
):
    me = lax.axis_index("pts")
    br = lax.axis_index("branch")
    nodes_here = sq_ref.shape[0]
    node_total = shards * nodes_here
    block_total = owner_ref.shape[1]
    nb = block_total // shards
    anchors = anchor_ref.shape[1]
    half = nb // 2

    loads = []
    for i, (src, dst) in enumerate(
        ((pf_hbm, pf), (qf_hbm, qf), (w_q_hbm, w_q), (w_mid_hbm, w_mid), (w_kv_hbm, w_kv), (w_out_hbm, w_out))
    ):
        copy = pltpu.make_async_copy(src, dst, load_sem.at[i])
        copy.start()
        loads.append(copy)

    barrier = pltpu.get_barrier_semaphore()
    for k in range(1, shards):
        pl.semaphore_signal(
            barrier, inc=1, device_id={"pts": lax.rem(me + k, shards)}, device_id_type=MESH
        )
    pl.semaphore_signal(barrier, inc=1, device_id={"branch": 1 - br}, device_id_type=MESH)
    pl.semaphore_wait(barrier, shards)

    def q_copy(k, row):
        place = all_q.at[pl.ds(pl.multiple_of(row * nodes_here, nodes_here), nodes_here)]
        return pltpu.make_async_remote_copy(
            src_ref=sq_ref,
            dst_ref=place,
            send_sem=q_send.at[k],
            recv_sem=q_recv.at[row],
            device_id={"pts": lax.rem(me + k, shards)},
            device_id_type=MESH,
        )

    def p_copy(c, k, row):
        place = all_p.at[pl.ds(pl.multiple_of(row * nb + c * half, half), half)]
        return pltpu.make_async_remote_copy(
            src_ref=place,
            dst_ref=place,
            send_sem=p_send.at[c, k],
            recv_sem=p_recv.at[c, row],
            device_id={"pts": lax.rem(me + k, shards)},
            device_id_type=MESH,
        )

    for k in range(1, shards):
        q_copy(k, me).start()
    all_q[pl.ds(pl.multiple_of(me * nodes_here, nodes_here), nodes_here), :] = sq_ref[...]

    w_half = w_in_ref[...] * jnp.asarray(0.5, BF)
    gain = math.sqrt(2.0 / math.pi)
    loads[0].wait()
    rows = 512

    def encode(i, carry):
        at = pl.ds(pl.multiple_of(i * rows, rows), rows)
        y = nn(pf[at, :], w_half)
        t = jnp.tanh(y * (2.0 * gain + (8.0 * 0.044715 * gain) * (y * y)))
        hid[at, :] = (y + y * t).astype(BF)
        return carry

    lax.fori_loop(0, nb * BLK // rows, encode, 0)

    loads[1].wait()
    loads[2].wait()
    scale = math.log2(math.e) / math.sqrt(HS)
    queries[...] = (nn(qf[...], w_q[...]) * scale).astype(BF)

    ids_row = owner_ref[...] * nodes_here + slot_ref[...]
    my_ids = jnp.sum(
        jnp.where(
            iota((nb, block_total), 1) == iota((nb, block_total), 0) + me * nb, ids_row, 0
        ).astype(F32),
        axis=1,
        keepdims=True,
    ).astype(jnp.int32)
    anchor_col = jnp.sum(
        jnp.where(
            iota((anchors, anchors), 1) == iota((anchors, anchors), 0), anchor_ref[...], 0
        ).astype(F32),
        axis=1,
        keepdims=True,
    ).astype(jnp.int32)
    pick_block = (iota((nb, node_total), 1) == my_ids).astype(F32).astype(BF)

    loads[3].wait()
    for k in range(1, shards):
        q_copy(k, lax.rem(me + shards - k, shards)).wait_recv()

    block_q = nn(pick_block, all_q[...])
    own_head = iota((HP, D), 1) // HS == iota((HP, D), 0)
    for c in range(2):
        asked = jnp.where(
            own_head[None], block_q[c * half : (c + 1) * half][:, None, :], 0.0
        ).reshape(half * HP, D)
        u_s[...] = (nt(asked.astype(BF), w_mid[...]) / math.sqrt(HS)).astype(BF)
        for n in range(half):
            rows_n = hid[pl.ds((c * half + n) * BLK, BLK), :]
            s_s[pl.ds(n * HP, HP), :] = nt(u_s[pl.ds(n * HP, HP), :], rows_n)
        scores = s_s[...]
        e = jnp.exp(scores - jnp.max(scores, axis=1, keepdims=True))
        weights = (e / jnp.sum(e, axis=1, keepdims=True)).astype(BF)
        for n in range(half):
            rows_n = hid[pl.ds((c * half + n) * BLK, BLK), :]
            g_s[pl.ds(n * HP, HP), :] = nn(weights[n * HP : (n + 1) * HP], rows_n).astype(BF)
        mixed = nn(g_s[...], w_mid[...]).reshape(half, HP, D)
        pooled = jnp.sum(jnp.where(own_head[None], mixed, 0.0), axis=1).astype(BF)
        all_p[pl.ds(pl.multiple_of(me * nb + c * half, half), half), :] = pooled
        for k in range(1, shards):
            p_copy(c, k, me).start()

    member = (anchor_col == ids_row).astype(F32)
    count = jnp.sum(member, axis=1, keepdims=True)
    pick_node = (iota((anchors, node_total), 1) == anchor_col).astype(F32).astype(BF)
    anchor_q = nn(pick_node, all_q[...])
    loads[4].wait()
    for c in range(2):
        for k in range(1, shards):
            p_copy(c, k, lax.rem(me + shards - k, shards)).wait_recv()
    pooled_sum = nn(member.astype(BF), all_p[...])
    v = anchor_q + pooled_sum / jnp.maximum(count, 1.0)
    feat = (v * lax.rsqrt(jnp.mean(v * v, axis=1, keepdims=True) + 1e-06)).astype(BF)
    kv_own[...] = nn(feat, w_kv[...]).astype(BF)
    swap = pltpu.make_async_remote_copy(
        src_ref=kv_own,
        dst_ref=kv_far,
        send_sem=kv_send,
        recv_sem=kv_recv,
        device_id={"branch": 1 - br},
        device_id_type=MESH,
    )
    swap.start()

    lane = iota((anchors, LANES), 1) // HS

    def attend(kv, base):
        for g in range(D // LANES):
            at = pl.ds(g * LANES, LANES)
            q = queries[:, at]
            keys = kv[:, at]
            values = kv[:, pl.ds(D + g * LANES, LANES)]
            total = None
            for h in range(LANES // HS):
                mine = lane == h
                zero = jnp.zeros_like(keys)
                s = nt(q, jnp.where(mine, keys, zero))
                p = jnp.exp2(s - jnp.max(s, axis=1, keepdims=True)).astype(BF)
                wide = jnp.concatenate(
                    [jnp.where(mine, values, zero), jnp.where(mine, 1.0, 0.0).astype(BF)], axis=1
                )
                part = nn(p, wide)
                total = part if total is None else total + part
            joined[:, pl.ds(base + g * LANES, LANES)] = (
                total[:, :LANES] / total[:, LANES:]
            ).astype(BF)

    attend(kv_own, 0)
    swap.wait()
    attend(kv_far, D)
    loads[5].wait()
    out_ref[...] = nn(joined[...], w_out[...]).astype(BF)

    for k in range(1, shards):
        q_copy(k, me).wait_send()
        for c in range(2):
            p_copy(c, k, me).wait_send()


def per_device(
    point_feat,
    query_feat,
    supernode_query,
    route_owner,
    route_slot,
    anchor_index,
    w_in,
    w_mid,
    w_q,
    w_kv,
    w_out,
):
    shards = lax.axis_size("pts")
    points = point_feat[0]
    rows = query_feat.shape[1]
    nodes = supernode_query.shape[1] * shards
    blocks = route_slot.shape[1]
    half = blocks // shards // 2
    anchors = anchor_index.shape[1]
    vmem = pl.BlockSpec(memory_space=pltpu.VMEM)
    hbm = pl.BlockSpec(memory_space=pl.ANY)
    result = pl.pallas_call(
        functools.partial(kernel, shards),
        out_shape=jax.ShapeDtypeStruct((rows, D), BF),
        in_specs=[vmem] * 5 + [hbm] * 6,
        out_specs=vmem,
        scratch_shapes=[
            pltpu.VMEM(points.shape, BF),
            pltpu.VMEM((rows, D), BF),
            pltpu.VMEM((D, D), BF),
            pltpu.VMEM((D, D), BF),
            pltpu.VMEM((D, 2 * D), BF),
            pltpu.VMEM((2 * D, D), BF),
            pltpu.VMEM((points.shape[0], D), BF),
            pltpu.VMEM((rows, D), BF),
            pltpu.VMEM((nodes, D), BF),
            pltpu.VMEM((blocks, D), BF),
            pltpu.VMEM((half * HP, D), BF),
            pltpu.VMEM((half * HP, BLK), F32),
            pltpu.VMEM((half * HP, D), BF),
            pltpu.VMEM((anchors, 2 * D), BF),
            pltpu.VMEM((anchors, 2 * D), BF),
            pltpu.VMEM((rows, 2 * D), BF),
            pltpu.SemaphoreType.DMA((6,)),
            pltpu.SemaphoreType.DMA((shards,)),
            pltpu.SemaphoreType.DMA((shards,)),
            pltpu.SemaphoreType.DMA((2, shards)),
            pltpu.SemaphoreType.DMA((2, shards)),
            pltpu.SemaphoreType.DMA,
            pltpu.SemaphoreType.DMA,
        ],
        compiler_params=pltpu.CompilerParams(
            collective_id=0, has_side_effects=True, vmem_limit_bytes=48 * 1024 * 1024
        ),
    )(
        supernode_query[0],
        route_owner[0].reshape(1, blocks),
        route_slot,
        anchor_index,
        w_in[0],
        points,
        query_feat[0],
        w_q[0],
        w_mid[0],
        w_kv[0],
        w_out[0],
    )
    return result[None]


def solution(mesh):
    return jax.shard_map(
        per_device,
        mesh=mesh,
        in_specs=(
            P("branch", ("groups", "pts"), None),
            P("branch", ("groups", "pts"), None),
            P("branch", ("groups", "pts"), None),
            P("branch", "groups", None),
            P("branch", "groups"),
            P("branch", "groups"),
            P("branch", None, None),
            P("branch", None, None),
            P("branch", None, None),
            P("branch", None, None),
            P("branch", None, None),
        ),
        out_specs=P("branch", ("groups", "pts"), None),
        check_vma=False,
    )
```

```python
import functools
import math

import jax
import jax.numpy as jnp
from jax import lax
from jax.experimental import pallas as pl
from jax.experimental.pallas import tpu as pltpu
from jax.sharding import PartitionSpec as P

D = 768
HEADS = 12
BLK = 128
HS = D // HEADS
LANES = 128
HP = 16
BF = jnp.bfloat16
F32 = jnp.float32
MESH = pl.DeviceIdType.MESH


def nn(a, b):
    return lax.dot_general(a, b, (((1,), (0,)), ((), ())), preferred_element_type=F32)


def nt(a, b):
    return lax.dot_general(a, b, (((1,), (1,)), ((), ())), preferred_element_type=F32)


def iota(shape, axis):
    return lax.broadcasted_iota(jnp.int32, shape, axis)


def kernel(
    shards,
    sq_hbm,
    owner_hbm,
    slot_hbm,
    anchor_hbm,
    w_in_hbm,
    pf_hbm,
    qf_hbm,
    w_q_hbm,
    w_mid_hbm,
    w_kv_hbm,
    w_out_hbm,
    out_ref,
    sq_ref,
    owner_ref,
    slot_ref,
    anchor_ref,
    w_in_ref,
    pf,
    qf,
    w_q,
    w_mid,
    w_kv,
    w_out,
    hid,
    queries,
    all_q,
    all_p,
    u_s,
    s_s,
    g_s,
    kv_own,
    kv_far,
    joined,
    load_sem,
    q_send,
    q_recv,
    p_send,
    p_recv,
    kv_send,
    kv_recv,
):
    me = lax.axis_index("pts")
    br = lax.axis_index("branch")
    nodes_here = sq_ref.shape[0]
    node_total = shards * nodes_here
    block_total = owner_ref.shape[1]
    nb = block_total // shards
    anchors = anchor_ref.shape[1]
    half = nb // 2

    loads = []
    for i, (src, dst) in enumerate(
        (
            (sq_hbm, sq_ref),
            (w_in_hbm, w_in_ref),
            (owner_hbm, owner_ref),
            (slot_hbm, slot_ref),
            (anchor_hbm, anchor_ref),
            (pf_hbm, pf),
            (qf_hbm, qf),
            (w_q_hbm, w_q),
            (w_mid_hbm, w_mid),
            (w_kv_hbm, w_kv),
            (w_out_hbm, w_out),
        )
    ):
        copy = pltpu.make_async_copy(src, dst, load_sem.at[i])
        copy.start()
        loads.append(copy)

    barrier = pltpu.get_barrier_semaphore()
    for k in range(1, shards):
        pl.semaphore_signal(
            barrier, inc=1, device_id={"pts": lax.rem(me + k, shards)}, device_id_type=MESH
        )
    pl.semaphore_signal(barrier, inc=1, device_id={"branch": 1 - br}, device_id_type=MESH)
    pl.semaphore_wait(barrier, shards)

    def q_copy(k, row):
        place = all_q.at[pl.ds(pl.multiple_of(row * nodes_here, nodes_here), nodes_here)]
        return pltpu.make_async_remote_copy(
            src_ref=sq_ref,
            dst_ref=place,
            send_sem=q_send.at[k],
            recv_sem=q_recv.at[row],
            device_id={"pts": lax.rem(me + k, shards)},
            device_id_type=MESH,
        )

    def p_copy(c, k, row):
        place = all_p.at[pl.ds(pl.multiple_of(row * nb + c * half, half), half)]
        return pltpu.make_async_remote_copy(
            src_ref=place,
            dst_ref=place,
            send_sem=p_send.at[c, k],
            recv_sem=p_recv.at[c, row],
            device_id={"pts": lax.rem(me + k, shards)},
            device_id_type=MESH,
        )

    loads[0].wait()
    for k in range(1, shards):
        q_copy(k, me).start()
    all_q[pl.ds(pl.multiple_of(me * nodes_here, nodes_here), nodes_here), :] = sq_ref[...]

    loads[1].wait()
    w_half = w_in_ref[...] * jnp.asarray(0.5, BF)
    gain = math.sqrt(2.0 / math.pi)
    loads[5].wait()
    rows = 512

    def encode(i, carry):
        at = pl.ds(pl.multiple_of(i * rows, rows), rows)
        y = nn(pf[at, :], w_half)
        t = jnp.tanh(y * (2.0 * gain + (8.0 * 0.044715 * gain) * (y * y)))
        hid[at, :] = (y + y * t).astype(BF)
        return carry

    lax.fori_loop(0, nb * BLK // rows, encode, 0)

    loads[6].wait()
    loads[7].wait()
    scale = math.log2(math.e) / math.sqrt(HS)
    queries[...] = (nn(qf[...], w_q[...]) * scale).astype(BF)

    for i in (2, 3, 4):
        loads[i].wait()
    ids_row = owner_ref[...] * nodes_here + slot_ref[...]
    my_ids = jnp.sum(
        jnp.where(
            iota((nb, block_total), 1) == iota((nb, block_total), 0) + me * nb, ids_row, 0
        ).astype(F32),
        axis=1,
        keepdims=True,
    ).astype(jnp.int32)
    anchor_col = jnp.sum(
        jnp.where(
            iota((anchors, anchors), 1) == iota((anchors, anchors), 0), anchor_ref[...], 0
        ).astype(F32),
        axis=1,
        keepdims=True,
    ).astype(jnp.int32)
    pick_block = (iota((nb, node_total), 1) == my_ids).astype(F32).astype(BF)

    loads[8].wait()
    for k in range(1, shards):
        q_copy(k, lax.rem(me + shards - k, shards)).wait_recv()

    block_q = nn(pick_block, all_q[...])
    own_head = iota((HP, D), 1) // HS == iota((HP, D), 0)
    for c in range(2):
        asked = jnp.where(
            own_head[None], block_q[c * half : (c + 1) * half][:, None, :], 0.0
        ).reshape(half * HP, D)
        u_s[...] = (nt(asked.astype(BF), w_mid[...]) / math.sqrt(HS)).astype(BF)
        for n in range(half):
            rows_n = hid[pl.ds((c * half + n) * BLK, BLK), :]
            s_s[pl.ds(n * HP, HP), :] = nt(u_s[pl.ds(n * HP, HP), :], rows_n)
        scores = s_s[...]
        e = jnp.exp(scores - jnp.max(scores, axis=1, keepdims=True))
        weights = (e / jnp.sum(e, axis=1, keepdims=True)).astype(BF)
        for n in range(half):
            rows_n = hid[pl.ds((c * half + n) * BLK, BLK), :]
            g_s[pl.ds(n * HP, HP), :] = nn(weights[n * HP : (n + 1) * HP], rows_n).astype(BF)
        mixed = nn(g_s[...], w_mid[...]).reshape(half, HP, D)
        pooled = jnp.sum(jnp.where(own_head[None], mixed, 0.0), axis=1).astype(BF)
        all_p[pl.ds(pl.multiple_of(me * nb + c * half, half), half), :] = pooled
        for k in range(1, shards):
            p_copy(c, k, me).start()

    member = (anchor_col == ids_row).astype(F32)
    count = jnp.sum(member, axis=1, keepdims=True)
    pick_node = (iota((anchors, node_total), 1) == anchor_col).astype(F32).astype(BF)
    anchor_q = nn(pick_node, all_q[...])
    loads[9].wait()
    for c in range(2):
        for k in range(1, shards):
            p_copy(c, k, lax.rem(me + shards - k, shards)).wait_recv()
    pooled_sum = nn(member.astype(BF), all_p[...])
    v = anchor_q + pooled_sum / jnp.maximum(count, 1.0)
    feat = (v * lax.rsqrt(jnp.mean(v * v, axis=1, keepdims=True) + 1e-06)).astype(BF)
    kv_own[...] = nn(feat, w_kv[...]).astype(BF)
    swap = pltpu.make_async_remote_copy(
        src_ref=kv_own,
        dst_ref=kv_far,
        send_sem=kv_send,
        recv_sem=kv_recv,
        device_id={"branch": 1 - br},
        device_id_type=MESH,
    )
    swap.start()

    lane = iota((anchors, LANES), 1) // HS

    def attend(kv, base):
        for g in range(D // LANES):
            at = pl.ds(g * LANES, LANES)
            q = queries[:, at]
            keys = kv[:, at]
            values = kv[:, pl.ds(D + g * LANES, LANES)]
            total = None
            for h in range(LANES // HS):
                mine = lane == h
                zero = jnp.zeros_like(keys)
                s = nt(q, jnp.where(mine, keys, zero))
                p = jnp.exp2(s - jnp.max(s, axis=1, keepdims=True)).astype(BF)
                wide = jnp.concatenate(
                    [jnp.where(mine, values, zero), jnp.where(mine, 1.0, 0.0).astype(BF)], axis=1
                )
                part = nn(p, wide)
                total = part if total is None else total + part
            joined[:, pl.ds(base + g * LANES, LANES)] = (
                total[:, :LANES] / total[:, LANES:]
            ).astype(BF)

    attend(kv_own, 0)
    swap.wait()
    attend(kv_far, D)
    loads[10].wait()
    out_ref[...] = nn(joined[...], w_out[...]).astype(BF)

    for k in range(1, shards):
        q_copy(k, me).wait_send()
        for c in range(2):
            p_copy(c, k, me).wait_send()


def per_device(
    point_feat,
    query_feat,
    supernode_query,
    route_owner,
    route_slot,
    anchor_index,
    w_in,
    w_mid,
    w_q,
    w_kv,
    w_out,
):
    shards = lax.axis_size("pts")
    points = point_feat[0]
    rows = query_feat.shape[1]
    nodes = supernode_query.shape[1] * shards
    blocks = route_slot.shape[1]
    half = blocks // shards // 2
    anchors = anchor_index.shape[1]
    vmem = pl.BlockSpec(memory_space=pltpu.VMEM)
    hbm = pl.BlockSpec(memory_space=pltpu.HBM)
    result = pl.pallas_call(
        functools.partial(kernel, shards),
        out_shape=jax.ShapeDtypeStruct((rows, D), BF),
        in_specs=[hbm] * 11,
        out_specs=vmem,
        scratch_shapes=[
            pltpu.VMEM(supernode_query.shape[1:], BF),
            pltpu.VMEM((1, blocks), jnp.int32),
            pltpu.VMEM((1, blocks), jnp.int32),
            pltpu.VMEM((1, anchors), jnp.int32),
            pltpu.VMEM(w_in.shape[1:], BF),
            pltpu.VMEM(points.shape, BF),
            pltpu.VMEM((rows, D), BF),
            pltpu.VMEM((D, D), BF),
            pltpu.VMEM((D, D), BF),
            pltpu.VMEM((D, 2 * D), BF),
            pltpu.VMEM((2 * D, D), BF),
            pltpu.VMEM((points.shape[0], D), BF),
            pltpu.VMEM((rows, D), BF),
            pltpu.VMEM((nodes, D), BF),
            pltpu.VMEM((blocks, D), BF),
            pltpu.VMEM((half * HP, D), BF),
            pltpu.VMEM((half * HP, BLK), F32),
            pltpu.VMEM((half * HP, D), BF),
            pltpu.VMEM((anchors, 2 * D), BF),
            pltpu.VMEM((anchors, 2 * D), BF),
            pltpu.VMEM((rows, 2 * D), BF),
            pltpu.SemaphoreType.DMA((11,)),
            pltpu.SemaphoreType.DMA((shards,)),
            pltpu.SemaphoreType.DMA((shards,)),
            pltpu.SemaphoreType.DMA((2, shards)),
            pltpu.SemaphoreType.DMA((2, shards)),
            pltpu.SemaphoreType.DMA,
            pltpu.SemaphoreType.DMA,
        ],
        compiler_params=pltpu.CompilerParams(
            collective_id=0, has_side_effects=True, vmem_limit_bytes=60 * 1024 * 1024
        ),
    )(
        supernode_query[0],
        route_owner[0].reshape(1, blocks),
        route_slot,
        anchor_index,
        w_in[0],
        points,
        query_feat[0],
        w_q[0],
        w_mid[0],
        w_kv[0],
        w_out[0],
    )
    return result[None]


def solution(mesh):
    return jax.shard_map(
        per_device,
        mesh=mesh,
        in_specs=(
            P("branch", ("groups", "pts"), None),
            P("branch", ("groups", "pts"), None),
            P("branch", ("groups", "pts"), None),
            P("branch", "groups", None),
            P("branch", "groups"),
            P("branch", "groups"),
            P("branch", None, None),
            P("branch", None, None),
            P("branch", None, None),
            P("branch", None, None),
            P("branch", None, None),
        ),
        out_specs=P("branch", ("groups", "pts"), None),
        check_vma=False,
    )
```

```python
import functools
import math

import jax
import jax.numpy as jnp
from jax import lax
from jax.experimental import pallas as pl
from jax.experimental.pallas import tpu as pltpu
from jax.sharding import PartitionSpec as P

D = 768
HEADS = 12
BLK = 128
HS = D // HEADS
LANES = 128
HP = 16
BF = jnp.bfloat16
F32 = jnp.float32
MESH = pl.DeviceIdType.MESH


def nn(a, b):
    return lax.dot_general(a, b, (((1,), (0,)), ((), ())), preferred_element_type=F32)


def nt(a, b):
    return lax.dot_general(a, b, (((1,), (1,)), ((), ())), preferred_element_type=F32)


def iota(shape, axis):
    return lax.broadcasted_iota(jnp.int32, shape, axis)


def kernel(
    shards,
    sq_hbm,
    owner_hbm,
    slot_hbm,
    anchor_hbm,
    w_in_hbm,
    pf_hbm,
    qf_hbm,
    w_q_hbm,
    w_mid_hbm,
    w_kv_hbm,
    joined,
    sq_ref,
    owner_ref,
    slot_ref,
    anchor_ref,
    w_in_ref,
    pf,
    qf,
    w_q,
    w_mid,
    w_kv,
    hid,
    queries,
    all_q,
    all_p,
    u_s,
    s_s,
    g_s,
    kv_own,
    kv_far,
    load_sem,
    q_send,
    q_recv,
    p_send,
    p_recv,
    kv_send,
    kv_recv,
):
    me = lax.axis_index("pts")
    br = lax.axis_index("branch")
    nodes_here = sq_ref.shape[0]
    node_total = shards * nodes_here
    block_total = owner_ref.shape[1]
    nb = block_total // shards
    anchors = anchor_ref.shape[1]
    half = nb // 2

    loads = []
    for i, (src, dst) in enumerate(
        (
            (sq_hbm, sq_ref),
            (w_in_hbm, w_in_ref),
            (owner_hbm, owner_ref),
            (slot_hbm, slot_ref),
            (anchor_hbm, anchor_ref),
            (pf_hbm, pf),
            (qf_hbm, qf),
            (w_q_hbm, w_q),
            (w_mid_hbm, w_mid),
            (w_kv_hbm, w_kv),
        )
    ):
        copy = pltpu.make_async_copy(src, dst, load_sem.at[i])
        copy.start()
        loads.append(copy)

    barrier = pltpu.get_barrier_semaphore()
    for k in range(1, shards):
        pl.semaphore_signal(
            barrier, inc=1, device_id={"pts": lax.rem(me + k, shards)}, device_id_type=MESH
        )
    pl.semaphore_signal(barrier, inc=1, device_id={"branch": 1 - br}, device_id_type=MESH)
    pl.semaphore_wait(barrier, shards)

    def q_copy(k, row):
        place = all_q.at[pl.ds(pl.multiple_of(row * nodes_here, nodes_here), nodes_here)]
        return pltpu.make_async_remote_copy(
            src_ref=sq_ref,
            dst_ref=place,
            send_sem=q_send.at[k],
            recv_sem=q_recv.at[row],
            device_id={"pts": lax.rem(me + k, shards)},
            device_id_type=MESH,
        )

    def p_copy(c, k, row):
        place = all_p.at[pl.ds(pl.multiple_of(row * nb + c * half, half), half)]
        return pltpu.make_async_remote_copy(
            src_ref=place,
            dst_ref=place,
            send_sem=p_send.at[c, k],
            recv_sem=p_recv.at[c, row],
            device_id={"pts": lax.rem(me + k, shards)},
            device_id_type=MESH,
        )

    loads[0].wait()
    for k in range(1, shards):
        q_copy(k, me).start()
    all_q[pl.ds(pl.multiple_of(me * nodes_here, nodes_here), nodes_here), :] = sq_ref[...]

    loads[1].wait()
    w_half = w_in_ref[...] * jnp.asarray(0.5, BF)
    gain = math.sqrt(2.0 / math.pi)
    loads[5].wait()
    rows = 512

    def encode(i, carry):
        at = pl.ds(pl.multiple_of(i * rows, rows), rows)
        y = nn(pf[at, :], w_half)
        t = jnp.tanh(y * (2.0 * gain + (8.0 * 0.044715 * gain) * (y * y)))
        hid[at, :] = (y + y * t).astype(BF)
        return carry

    lax.fori_loop(0, nb * BLK // rows, encode, 0)

    for i in (2, 3, 4):
        loads[i].wait()
    ids_row = owner_ref[...] * nodes_here + slot_ref[...]
    my_ids = jnp.sum(
        jnp.where(
            iota((nb, block_total), 1) == iota((nb, block_total), 0) + me * nb, ids_row, 0
        ).astype(F32),
        axis=1,
        keepdims=True,
    ).astype(jnp.int32)
    anchor_col = jnp.sum(
        jnp.where(
            iota((anchors, anchors), 1) == iota((anchors, anchors), 0), anchor_ref[...], 0
        ).astype(F32),
        axis=1,
        keepdims=True,
    ).astype(jnp.int32)
    pick_block = (iota((nb, node_total), 1) == my_ids).astype(F32).astype(BF)

    loads[8].wait()
    for k in range(1, shards):
        q_copy(k, lax.rem(me + shards - k, shards)).wait_recv()

    block_q = nn(pick_block, all_q[...])
    own_head = iota((HP, D), 1) // HS == iota((HP, D), 0)
    for c in range(2):
        asked = jnp.where(
            own_head[None], block_q[c * half : (c + 1) * half][:, None, :], 0.0
        ).reshape(half * HP, D)
        u_s[...] = (nt(asked.astype(BF), w_mid[...]) / math.sqrt(HS)).astype(BF)
        for n in range(half):
            rows_n = hid[pl.ds((c * half + n) * BLK, BLK), :]
            s_s[pl.ds(n * HP, HP), :] = nt(u_s[pl.ds(n * HP, HP), :], rows_n)
        scores = s_s[...]
        e = jnp.exp(scores - jnp.max(scores, axis=1, keepdims=True))
        weights = (e / jnp.sum(e, axis=1, keepdims=True)).astype(BF)
        for n in range(half):
            rows_n = hid[pl.ds((c * half + n) * BLK, BLK), :]
            g_s[pl.ds(n * HP, HP), :] = nn(weights[n * HP : (n + 1) * HP], rows_n).astype(BF)
        mixed = nn(g_s[...], w_mid[...]).reshape(half, HP, D)
        pooled = jnp.sum(jnp.where(own_head[None], mixed, 0.0), axis=1).astype(BF)
        all_p[pl.ds(pl.multiple_of(me * nb + c * half, half), half), :] = pooled
        for k in range(1, shards):
            p_copy(c, k, me).start()

    member = (anchor_col == ids_row).astype(F32)
    count = jnp.sum(member, axis=1, keepdims=True)
    pick_node = (iota((anchors, node_total), 1) == anchor_col).astype(F32).astype(BF)
    anchor_q = nn(pick_node, all_q[...])
    loads[6].wait()
    loads[7].wait()
    scale = math.log2(math.e) / math.sqrt(HS)
    queries[...] = (nn(qf[...], w_q[...]) * scale).astype(BF)

    loads[9].wait()
    for c in range(2):
        for k in range(1, shards):
            p_copy(c, k, lax.rem(me + shards - k, shards)).wait_recv()
    pooled_sum = nn(member.astype(BF), all_p[...])
    v = anchor_q + pooled_sum / jnp.maximum(count, 1.0)
    feat = (v * lax.rsqrt(jnp.mean(v * v, axis=1, keepdims=True) + 1e-06)).astype(BF)
    kv_own[...] = nn(feat, w_kv[...]).astype(BF)
    swap = pltpu.make_async_remote_copy(
        src_ref=kv_own,
        dst_ref=kv_far,
        send_sem=kv_send,
        recv_sem=kv_recv,
        device_id={"branch": 1 - br},
        device_id_type=MESH,
    )
    swap.start()

    lane = iota((anchors, LANES), 1) // HS

    def attend(kv, base):
        for g in range(D // LANES):
            at = pl.ds(g * LANES, LANES)
            q = queries[:, at]
            keys = kv[:, at]
            values = kv[:, pl.ds(D + g * LANES, LANES)]
            total = None
            for h in range(LANES // HS):
                mine = lane == h
                zero = jnp.zeros_like(keys)
                s = nt(q, jnp.where(mine, keys, zero))
                p = jnp.exp2(s - jnp.max(s, axis=1, keepdims=True)).astype(BF)
                wide = jnp.concatenate(
                    [jnp.where(mine, values, zero), jnp.where(mine, 1.0, 0.0).astype(BF)], axis=1
                )
                part = nn(p, wide)
                total = part if total is None else total + part
            joined[:, pl.ds(base + g * LANES, LANES)] = (
                total[:, :LANES] / total[:, LANES:]
            ).astype(BF)

    attend(kv_own, 0)
    swap.wait()
    attend(kv_far, D)

    for k in range(1, shards):
        q_copy(k, me).wait_send()
        for c in range(2):
            p_copy(c, k, me).wait_send()


def per_device(
    point_feat,
    query_feat,
    supernode_query,
    route_owner,
    route_slot,
    anchor_index,
    w_in,
    w_mid,
    w_q,
    w_kv,
    w_out,
):
    shards = lax.axis_size("pts")
    points = point_feat[0]
    rows = query_feat.shape[1]
    nodes = supernode_query.shape[1] * shards
    blocks = route_slot.shape[1]
    half = blocks // shards // 2
    anchors = anchor_index.shape[1]
    vmem = pl.BlockSpec(memory_space=pltpu.VMEM)
    hbm = pl.BlockSpec(memory_space=pltpu.HBM)
    both = pl.pallas_call(
        functools.partial(kernel, shards),
        out_shape=jax.ShapeDtypeStruct((rows, 2 * D), BF),
        in_specs=[hbm] * 10,
        out_specs=vmem,
        scratch_shapes=[
            pltpu.VMEM(supernode_query.shape[1:], BF),
            pltpu.VMEM((1, blocks), jnp.int32),
            pltpu.VMEM((1, blocks), jnp.int32),
            pltpu.VMEM((1, anchors), jnp.int32),
            pltpu.VMEM(w_in.shape[1:], BF),
            pltpu.VMEM(points.shape, BF),
            pltpu.VMEM((rows, D), BF),
            pltpu.VMEM((D, D), BF),
            pltpu.VMEM((D, D), BF),
            pltpu.VMEM((D, 2 * D), BF),
            pltpu.VMEM((points.shape[0], D), BF),
            pltpu.VMEM((rows, D), BF),
            pltpu.VMEM((nodes, D), BF),
            pltpu.VMEM((blocks, D), BF),
            pltpu.VMEM((half * HP, D), BF),
            pltpu.VMEM((half * HP, BLK), F32),
            pltpu.VMEM((half * HP, D), BF),
            pltpu.VMEM((anchors, 2 * D), BF),
            pltpu.VMEM((anchors, 2 * D), BF),
            pltpu.SemaphoreType.DMA((10,)),
            pltpu.SemaphoreType.DMA((shards,)),
            pltpu.SemaphoreType.DMA((shards,)),
            pltpu.SemaphoreType.DMA((2, shards)),
            pltpu.SemaphoreType.DMA((2, shards)),
            pltpu.SemaphoreType.DMA,
            pltpu.SemaphoreType.DMA,
        ],
        compiler_params=pltpu.CompilerParams(
            collective_id=0, has_side_effects=True, vmem_limit_bytes=60 * 1024 * 1024
        ),
    )(
        supernode_query[0],
        route_owner[0].reshape(1, blocks),
        route_slot,
        anchor_index,
        w_in[0],
        points,
        query_feat[0],
        w_q[0],
        w_mid[0],
        w_kv[0],
    )
    return nn(both, w_out[0]).astype(BF)[None]


def solution(mesh):
    return jax.shard_map(
        per_device,
        mesh=mesh,
        in_specs=(
            P("branch", ("groups", "pts"), None),
            P("branch", ("groups", "pts"), None),
            P("branch", ("groups", "pts"), None),
            P("branch", "groups", None),
            P("branch", "groups"),
            P("branch", "groups"),
            P("branch", None, None),
            P("branch", None, None),
            P("branch", None, None),
            P("branch", None, None),
            P("branch", None, None),
        ),
        out_specs=P("branch", ("groups", "pts"), None),
        check_vma=False,
    )
```
